128 devices in a mesh: src: 8 (over z_lo, x), tgt: 16 (over y, z_hi, core).
Axes of the slice: x: 4, y: 4, z: 4 (z_hi: 2, z_lo: 2; z = z_hi * 2 + z_lo), core: 2. Of those that a mesh axis runs over, the one named last changes fastest.
Arguments:
- src_values: float32 [16, 131072], P(None, ('src', 'tgt')), may hold values from -6 to 6
- src_offset: float32 [131072], P(('src', 'tgt')), may hold values from -1 to 1
- src_box: int32 [131072], P(('src', 'tgt')), may hold values from 0 to 32767, as said below
- tgt_offset: float32 [131072], P(('src', 'tgt')), may hold values from -1 to 1
- tgt_box: int32 [131072], P(('src', 'tgt')), may hold values from 0 to 32767, as said below
- pattern: int32 [15, 32768], P(None, ('src', 'tgt')), may hold values from 0 to 3
- operators: float32 [15, 4, 2, 64, 128], replicated, may hold values from -0.5 to 0.5
Outputs:
- target_values: float32 [16, 131072], P(None, ('src', 'tgt'))
The draws below stay inside these ranges and needn't reach their ends.
Inputs may be any that keep to these rules, and one draw needn't show every extreme that they name: `src_box`: source point p lies in a box of the block [(p // 1024) * 256, (p // 1024 + 1) * 256). `tgt_box`: target point q lies in a box of the block [(q // 1024) * 256, (q // 1024 + 1) * 256).
All inputs are finite; a program needn't handle non-finite values.
Results may differ from the reference program's by a relative error of at most 0.00016.
Values sent between devices are 32-bit elements; how exact they have to be, the bound alone decides.
A program may use at most 128 MiB of HBM per device.

```python
import jax
import jax.numpy as jnp
from jax import lax

RANK = 64
KINDS = 4
FUNCS = 16
NPTS_DEV = 1024
LEVELS = 15
BOXES_DEV = 256
BOXES = 32768
NPTS = 131072


def draw_src_box(key, part):
    key = jax.random.fold_in(key, 11)
    block = jnp.arange(NPTS, dtype=jnp.int32) // NPTS_DEV
    inside = jax.random.randint(key, (NPTS,), 0, BOXES_DEV, dtype=jnp.int32)
    return (block * BOXES_DEV + inside).astype(jnp.int32)


def draw_tgt_box(key, part):
    key = jax.random.fold_in(key, 23)
    block = jnp.arange(NPTS, dtype=jnp.int32) // NPTS_DEV
    inside = jax.random.randint(key, (NPTS,), 0, BOXES_DEV, dtype=jnp.int32)
    return (block * BOXES_DEV + inside).astype(jnp.int32)


def with_ends(drawn, key, low, high):
    extent = drawn.shape
    spot = [jax.random.randint(jax.random.fold_in(key, axis), (), 0, extent[axis]) for axis in range(len(extent))]
    drawn = drawn.at[tuple(spot)].set(low)
    longest = extent.index(max(extent))
    spot[longest] = (spot[longest] + 1) % extent[longest]
    return drawn.at[tuple(spot)].set(high)


def levels(rng, extent, cuts, smallest, top_value):
    loudness = 1.0
    for position, blocks in cuts:
        draws = jax.random.uniform(jax.random.fold_in(jax.random.fold_in(rng, 6), position), (blocks,), jnp.float32, smallest / len(cuts), top_value / len(cuts))
        loudness = loudness * jnp.repeat(jnp.exp(draws), extent[position] // blocks).reshape((-1,) + (1,) * (len(extent) - 1 - position))
    return loudness


def bell_draw(key, extent, spread, reach, cuts=(), kind=jnp.bfloat16):
    values = jax.random.normal(key, extent, jnp.float32) * spread
    if len(cuts) > 0:
        values = levels(key, extent, cuts, -0.22, 0.18) * values
    return jnp.clip(values, min=-reach, max=reach).astype(kind)


def setup_inputs(seed: int = 0) -> dict:
    arg_keys = jax.random.split(jax.random.key(seed), 8)
    src_values = bell_draw(arg_keys[0], (FUNCS, NPTS), 1.0, 6.0, ((1, 128),), jnp.float32)
    src_offset = jnp.clip(jax.random.uniform(arg_keys[1], (NPTS,), jnp.float32, -1.0, 1.0) * levels(arg_keys[1], (NPTS,), ((0, 128),), -0.4, 0.0), -1.0, 1.0)
    src_box = draw_src_box(jax.random.fold_in(arg_keys[7], 71), 0)
    tgt_offset = jnp.clip(jax.random.uniform(arg_keys[3], (NPTS,), jnp.float32, -1.0, 1.0) * levels(arg_keys[3], (NPTS,), ((0, 128),), -0.4, 0.0), -1.0, 1.0)
    tgt_box = draw_tgt_box(jax.random.fold_in(arg_keys[7], 71), 0)
    pattern = with_ends(jax.random.randint(arg_keys[5], (LEVELS, BOXES), 0, KINDS), jax.random.fold_in(arg_keys[5], 1), 0, KINDS - 1).astype(jnp.int32)
    operators = bell_draw(arg_keys[6], (LEVELS, KINDS, 2, RANK, 2 * RANK), (2 * RANK) ** -0.5, 0.5, (), jnp.float32)
    return {"src_values": src_values, "src_offset": src_offset, "src_box": src_box, "tgt_offset": tgt_offset, "tgt_box": tgt_box, "pattern": pattern, "operators": operators}


HIGHEST = lax.Precision.HIGHEST


def chebyshev(points):
    rows = [jnp.ones_like(points), points]
    for order in range(2, RANK):
        rows.append(2.0 * points * rows[-1] - rows[-2])
    return jnp.stack(rows[:RANK])


def apply_level(coefficients, weights, pattern_row, bit_pos):
    count = coefficients.shape[1]
    outer = count >> (bit_pos + 1)
    inner = 1 << bit_pos
    split = coefficients.reshape(RANK, outer, 2, inner)
    stacked = jnp.concatenate([split[:, :, 0, :], split[:, :, 1, :]], axis=0)
    matrix = weights.reshape(KINDS * 2 * RANK, 2 * RANK)
    products = jnp.einsum("mr,rgh->mgh", matrix, stacked, precision=HIGHEST)
    products = products.reshape(KINDS, 2, RANK, outer, inner)
    kinds_row = jnp.arange(KINDS, dtype=jnp.int32)
    selector = (pattern_row.reshape(outer, 2, inner)[None] == kinds_row[:, None, None, None]).astype(jnp.float32)
    merged = jnp.einsum("kgch,kcrgh->rgch", selector, products, precision=HIGHEST)
    return merged.reshape(RANK, count)


def reference(src_values, src_offset, src_box, tgt_offset, tgt_box, pattern, operators):
    basis_src = chebyshev(src_offset)
    basis_tgt = chebyshev(tgt_offset)

    def one_function(values):
        weighted = (basis_src * values[None, :]).T
        coefficients = jax.ops.segment_sum(weighted, src_box, num_segments=BOXES).T
        for level in range(LEVELS):
            coefficients = apply_level(coefficients, operators[level], pattern[level], level)
        order = (0,) + tuple(range(LEVELS, 0, -1))
        final = coefficients.reshape((RANK,) + (2,) * LEVELS).transpose(order).reshape(RANK, BOXES)
        gathered = final[:, tgt_box]
        return 0.125 * jnp.sum(basis_tgt * gathered, axis=0)

    return lax.map(one_function, src_values)
```

```python
import functools

import jax
import jax.numpy as jnp
from jax import lax
from jax.experimental import pallas as pl
from jax.experimental.pallas import tpu as pltpu
from jax.sharding import PartitionSpec as P

RANK = 64
KINDS = 4
LANES = 2 * RANK
MESH = pl.DeviceIdType.MESH
F32, BF16 = jnp.float32, jnp.bfloat16
NT = (((1,), (1,)), ((), ()))
NN = (((1,), (0,)), ((), ()))


def split(x):
    hi = x.astype(BF16)
    return hi, (x - hi.astype(F32)).astype(BF16)


def dot(a, b, dims):
    return lax.dot_general(a, b, dims, preferred_element_type=F32)


def bit(x, k):
    return (x >> k) & 1


def reverse7(x):
    return sum(bit(x, k) << (6 - k) for k in range(7))


def reverse7_scalar(x):
    return sum(((x // 2**k) % 2) * 2 ** (6 - k) for k in range(7))


def row_of(box, level):
    parts = [bit(box, level - 1 - k) << k for k in range(level)]
    parts += [bit(box, 7 + level - k) << k for k in range(level, 7)]
    return sum(parts)


def chebyshev(points):
    n = points.shape[1]
    x = jnp.broadcast_to(points, (8, n))
    rows = [jnp.ones_like(x), x]
    for _ in range(7):
        rows.append(2.0 * x * rows[-1] - rows[-2])
    at = lax.broadcasted_iota(jnp.int32, (8, n), 0)
    now, before = rows[0], rows[8]
    for k in range(1, 8):
        now = jnp.where(at == k, rows[k], now)
        before = jnp.where(at == k, rows[8 - k], before)
    twice = 2.0 * rows[8]
    blocks = [now]
    for _ in range(RANK // 8 - 1):
        now, before = twice * now - before, now
        blocks.append(now)
    return jnp.concatenate(blocks, axis=0)


def half_masks(basis, child):
    return jnp.concatenate([jnp.where(child == c, basis, 0.0) for c in range(2)], axis=0)


def kernel(
    funcs_part, parts, tgt_size, devices,
    values_ref, src_offset_ref, src_box_ref, tgt_offset_ref, tgt_box_ref, pattern_ref, weights_ref,
    out_ref,
    work, wide, kinds, basis_in, basis_out, sent, arrived, pattern_sent, pattern_arrived,
    send_sem, recv_sem, pattern_send_sem, pattern_recv_sem,
):
    V = funcs_part
    src_me, tgt_me = lax.axis_index("src"), lax.axis_index("tgt")
    me = src_me * tgt_size + tgt_me
    slot = reverse7_scalar(me)

    def peer(k):
        other = (me + k) % devices
        return other, (other // tgt_size, other % tgt_size)

    barrier = pltpu.get_barrier_semaphore()

    @pl.loop(1, devices)
    def _(k):
        pl.semaphore_signal(barrier, inc=1, device_id=peer(k)[1], device_id_type=MESH)

    lane_low = lax.broadcasted_iota(jnp.int32, (1, 1, LANES), 2) < RANK

    def set_kinds(index, level, values, order, order_rows):
        rows = lax.broadcasted_iota(jnp.int32, (128, 256), 0)
        picked = jnp.where(row_of(order, level) == rows, values, 0.0).astype(BF16)
        lane_child = (lax.broadcasted_iota(jnp.int32, (256, LANES), 1) >= RANK).astype(jnp.int32)
        spread = jnp.where(bit(order_rows, level) == lane_child, 1.0, 0.0).astype(BF16)
        kinds[index] = dot(picked, spread, NN)

    def exchange_store(y, ref):
        y = y.reshape(128, V, LANES)
        top, low = y[:64], y[64:]
        n0 = jnp.where(lane_low, top, pltpu.roll(low.reshape(64 * V, LANES), RANK, 1).reshape(64, V, LANES))
        n1 = jnp.where(lane_low, pltpu.roll(top.reshape(64 * V, LANES), RANK, 1).reshape(64, V, LANES), low)
        ref[...] = jnp.stack([n0, n1], axis=1).reshape(128 * V, LANES)

    def level_product(index, x):
        hi, lo = split(weights_ref[index])
        wide[:, :LANES] = hi
        wide[:, LANES : 2 * LANES] = hi
        wide[:, 2 * LANES :] = lo
        hi, lo = split(x)
        product = dot(jnp.concatenate([hi, lo, hi], axis=1), wide[...], NT).reshape(128, V, KINDS * LANES)
        kind = jnp.concatenate(
            [jnp.broadcast_to(kinds[index, pl.ds(g, 1), :], (V, LANES))[None] for g in range(128)], axis=0
        )
        y = product[:, :, :LANES]
        for k in range(1, KINDS):
            y = jnp.where(kind == float(k), product[:, :, k * LANES : (k + 1) * LANES], y)
        return y

    def inner_levels(first):
        @pl.loop(0, 6)
        def _(i):
            now = lax.rem(i, 2)
            exchange_store(level_product(first + i, work[now]), work.at[1 - now])

    order = lax.broadcasted_iota(jnp.int32, (1, 256), 1)
    order_rows = lax.broadcasted_iota(jnp.int32, (256, LANES), 0)
    for level in range(7):
        set_kinds(level, level, pattern_ref[level : level + 1, :].astype(F32), order, order_rows)
    rows = []
    for level in range(7, 15):
        row = pattern_ref[level : level + 1, :].astype(F32)
        rows += [row[:, :128], row[:, 128:]]
    rows = jnp.concatenate(rows + [jnp.zeros((128 - len(rows), 128), F32)], axis=0).astype(BF16)
    to_device = lax.broadcasted_iota(jnp.int32, (128, 128), 0)
    from_box = lax.broadcasted_iota(jnp.int32, (128, 128), 1)
    permute = jnp.where(reverse7(to_device) == from_box, 1.0, 0.0).astype(BF16)
    pattern_sent[...] = dot(permute, rows, NT)[:, None, :]

    src_box = src_box_ref[...]
    src_row = reverse7((src_box >> 1) & 127)
    hi, lo = split(half_masks(chebyshev(src_offset_ref[...]), src_box & 1))
    basis_in[:LANES] = hi
    basis_in[LANES:] = lo
    tgt_box = tgt_box_ref[...]
    tgt_row = (tgt_box >> 1) & 127
    hi, lo = split(half_masks(chebyshev(tgt_offset_ref[...]), tgt_box & 1))
    basis_out[:LANES] = hi
    basis_out[LANES : 2 * LANES] = hi
    basis_out[2 * LANES :] = lo

    def expand(part, ref):
        values = values_ref[part * V : (part + 1) * V, :]
        hi, lo = split(values)
        hi, lo = hi.astype(F32)[None], lo.astype(F32)[None]
        B = 64

        @pl.loop(0, 128 // B)
        def _(b):
            g = lax.broadcasted_iota(jnp.int32, (B, 1, 1), 0) + b * B
            here = src_row[None] == g
            a = jnp.where(here, hi, 0.0).reshape(B * V, -1).astype(BF16)
            total = dot(a, basis_in[...], NT)
            a = jnp.where(here, lo, 0.0).reshape(B * V, -1).astype(BF16)
            total += dot(a, basis_in[...], NT)
            ref[pl.ds(pl.multiple_of(b * B * V, 8), B * V), :] = total[:, :LANES] + total[:, LANES:]

    def evaluate(part, x):
        hi, lo = split(x)
        x = jnp.concatenate([hi, lo, hi], axis=1)
        n = tgt_row.shape[1]
        Q = 256
        for q in range(0, n, Q):
            h = dot(x, basis_out[:, q : q + Q], NN).reshape(128, V, Q)
            g = lax.broadcasted_iota(jnp.int32, (128, 1, 1), 0)
            total = jnp.sum(jnp.where(tgt_row[None, :, q : q + Q] == g, h, 0.0), axis=0)
            out_ref[part * V : (part + 1) * V, q : q + Q] = 0.125 * total

    def up(part):
        expand(part, work.at[0])
        inner_levels(0)
        exchange_store(level_product(6, work[0]), sent.at[part])

    def block_copy(part, k):
        other, device = peer(k)
        return pltpu.make_async_remote_copy(
            src_ref=sent.at[part, pl.ds(pl.multiple_of(other * V, 8), V)],
            dst_ref=arrived.at[part, pl.ds(pl.multiple_of(slot * V, 8), V)],
            send_sem=send_sem.at[part],
            recv_sem=recv_sem.at[part],
            device_id=device,
            device_id_type=MESH,
        )

    def pattern_copy(k):
        other, device = peer(k)
        return pltpu.make_async_remote_copy(
            src_ref=pattern_sent.at[other],
            dst_ref=pattern_arrived.at[me],
            send_sem=pattern_send_sem,
            recv_sem=pattern_recv_sem,
            device_id=device,
            device_id_type=MESH,
        )

    def send(part):
        @pl.loop(1, devices)
        def _(k):
            block_copy(part, k).start()

        arrived[part, pl.ds(pl.multiple_of(slot * V, 8), V)] = sent[part, pl.ds(pl.multiple_of(me * V, 8), V)]

    def wait_all(ref, sem):
        pltpu.make_async_copy(ref, ref, sem).wait()

    others = pl.ds(0, (devices - 1) * V)

    up(0)
    pl.semaphore_wait(barrier, devices - 1)

    @pl.loop(1, devices)
    def _(k):
        pattern_copy(k).start()

    pattern_arrived[me] = pattern_sent[me]
    send(0)
    for part in range(1, parts):
        up(part)
        send(part)

    wait_all(pattern_arrived.at[pl.ds(0, devices - 1)], pattern_recv_sem)
    got = pattern_arrived[:, 0, :].astype(BF16)
    pick = jnp.where(to_device == from_box, 1.0, 0.0).astype(BF16)
    got = dot(pick, got, NT)
    lanes = lax.broadcasted_iota(jnp.int32, (1, 256), 1)
    order = ((lanes & 127) << 1) + (lanes >> 7)
    order_rows = ((order_rows & 127) << 1) + (order_rows >> 7)
    for level in range(8):
        row = jnp.concatenate([got[2 * level : 2 * level + 1], got[2 * level + 1 : 2 * level + 2]], axis=1)
        set_kinds(7 + level, level, row, order, order_rows)

    for part in range(parts):
        wait_all(arrived.at[part, others], recv_sem.at[part])
        exchange_store(level_product(7, arrived[part]), work.at[0])
        inner_levels(8)
        evaluate(part, level_product(14, work[0]).reshape(128 * V, LANES))

    wait_all(pattern_sent.at[pl.ds(0, devices - 1)], pattern_send_sem)
    for part in range(parts):
        wait_all(sent.at[part, others], send_sem.at[part])


def solution(mesh):
    src_size, tgt_size = mesh.shape["src"], mesh.shape["tgt"]
    devices = src_size * tgt_size
    parts = 2

    def on_device(src_values, src_offset, src_box, tgt_offset, tgt_box, pattern, operators):
        funcs, points = src_values.shape
        V = funcs // parts
        rows = 128 * V
        vmem = pl.BlockSpec(memory_space=pltpu.VMEM)
        return pl.pallas_call(
            functools.partial(kernel, V, parts, tgt_size, devices),
            out_shape=jax.ShapeDtypeStruct((funcs, points), F32),
            in_specs=[vmem] * 7,
            out_specs=vmem,
            scratch_shapes=[
                pltpu.VMEM((2, rows, LANES), F32),
                pltpu.VMEM((KINDS * LANES, 3 * LANES), BF16),
                pltpu.VMEM((15, 128, LANES), F32),
                pltpu.VMEM((2 * LANES, points), BF16),
                pltpu.VMEM((3 * LANES, points), BF16),
                pltpu.VMEM((parts, rows, LANES), F32),
                pltpu.VMEM((parts, rows, LANES), F32),
                pltpu.VMEM((devices, 1, LANES), F32),
                pltpu.VMEM((devices, 1, LANES), F32),
                pltpu.SemaphoreType.DMA((parts,)),
                pltpu.SemaphoreType.DMA((parts,)),
                pltpu.SemaphoreType.DMA,
                pltpu.SemaphoreType.DMA,
            ],
            compiler_params=pltpu.CompilerParams(
                collective_id=0, has_side_effects=True, vmem_limit_bytes=56 * 2**20
            ),
        )(
            src_values,
            src_offset.reshape(1, points),
            src_box.reshape(1, points) & 255,
            tgt_offset.reshape(1, points),
            tgt_box.reshape(1, points) & 255,
            pattern,
            operators.reshape(15, KINDS * LANES, LANES),
        )

    placed = (
        P(None, ("src", "tgt")),
        P(("src", "tgt")),
        P(("src", "tgt")),
        P(("src", "tgt")),
        P(("src", "tgt")),
        P(None, ("src", "tgt")),
        P(),
    )
    return jax.shard_map(
        on_device, mesh=mesh, in_specs=placed, out_specs=P(None, ("src", "tgt")), check_vma=False
    )
```

```python
import functools

import jax
import jax.numpy as jnp
from jax import lax
from jax.experimental import pallas as pl
from jax.experimental.pallas import tpu as pltpu
from jax.sharding import PartitionSpec as P

RANK = 64
KINDS = 4
LANES = 2 * RANK
MESH = pl.DeviceIdType.MESH
F32, BF16 = jnp.float32, jnp.bfloat16
NT = (((1,), (1,)), ((), ()))
NN = (((1,), (0,)), ((), ()))


def split(x):
    hi = x.astype(BF16)
    return hi, (x - hi.astype(F32)).astype(BF16)


def dot(a, b, dims):
    return lax.dot_general(a, b, dims, preferred_element_type=F32)


def bit(x, k):
    return (x >> k) & 1


def reverse(x, n):
    return sum(bit(x, k) << (n - 1 - k) for k in range(n))


def row_of(box, level):
    if level == 7:
        return reverse(box & 127, 7)
    parts = [bit(box, level - 1 - k) << k for k in range(level)]
    parts += [bit(box, 6 + level - k) << k for k in range(level, 6)]
    return sum(parts) + (bit(box, 7) << 6)


def chebyshev(points):
    n = points.shape[1]
    x = jnp.broadcast_to(points, (8, n))
    rows = [jnp.ones_like(x), x]
    for _ in range(7):
        rows.append(2.0 * x * rows[-1] - rows[-2])
    at = lax.broadcasted_iota(jnp.int32, (8, n), 0)
    now, before = rows[0], rows[8]
    for k in range(1, 8):
        now = jnp.where(at == k, rows[k], now)
        before = jnp.where(at == k, rows[8 - k], before)
    twice = 2.0 * rows[8]
    blocks = [now]
    for _ in range(RANK // 8 - 1):
        now, before = twice * now - before, now
        blocks.append(now)
    return jnp.concatenate(blocks, axis=0)


def half_masks(basis, child):
    return jnp.concatenate([jnp.where(child == c, basis, 0.0) for c in range(2)], axis=0)


def kernel(
    V, parts, src_size, tgt_size,
    values_ref, src_offset_ref, src_box_ref, tgt_offset_ref, tgt_box_ref, pattern_ref, weights_ref,
    out_ref,
    weights, wide, kinds, work, basis_in, basis_out, sent, arrived,
    weights_sem, send_sem, recv_sem,
):
    devices = src_size * tgt_size
    levels = weights.shape[0]
    src_me, tgt_me = lax.axis_index("src"), lax.axis_index("tgt")
    me = src_me * tgt_size + tgt_me
    low, slot = lax.rem(me, 64), (me // 64) * 64
    for k in range(6):
        slot = slot + lax.rem(low // 2**k, 2) * 2 ** (5 - k)
    src_of = [lax.rem(src_me + k, src_size) for k in range(src_size)]
    tgt_of = [lax.rem(tgt_me + k, tgt_size) for k in range(tgt_size)]
    peers = [(s, t) for s in src_of for t in tgt_of][1:]

    def weights_copy(level):
        return pltpu.make_async_copy(weights_ref.at[level], weights.at[level], weights_sem.at[level])

    for level in range(levels):
        weights_copy(level).start()

    barrier = pltpu.get_barrier_semaphore()

    def greet(peer):
        pl.semaphore_signal(barrier, inc=1, device_id=peer, device_id_type=MESH)

    for peer in peers:
        greet(peer)

    def block_copy(part, peer):
        return pltpu.make_async_remote_copy(
            src_ref=sent[part].at[peer[0] * tgt_size + peer[1]],
            dst_ref=arrived[part].at[slot],
            send_sem=send_sem.at[part],
            recv_sem=recv_sem.at[part],
            device_id=peer,
            device_id_type=MESH,
        )

    lane_low = lax.broadcasted_iota(jnp.int32, (1, 1, LANES), 2) < RANK

    def set_kinds(index, level, values, order, order_rows):
        rows = lax.broadcasted_iota(jnp.int32, (128, 256), 0)
        picked = jnp.where(row_of(order, level) == rows, values, 0.0).astype(BF16)
        lane_child = (lax.broadcasted_iota(jnp.int32, (256, LANES), 1) >= RANK).astype(jnp.int32)
        spread = jnp.where(bit(order_rows, level) == lane_child, 1.0, 0.0).astype(BF16)
        kinds[index] = dot(picked, spread, NN)

    def exchange(y):
        n = y.shape[0]

        def turned(a):
            return pltpu.roll(a.reshape(n // 2 * V, LANES), RANK, 1).reshape(n // 2, V, LANES)

        top, low = y[: n // 2], y[n // 2 :]
        n0 = jnp.where(lane_low, top, turned(low))
        n1 = jnp.where(lane_low, turned(top), low)
        return jnp.stack([n0, n1], axis=1).reshape(n, V, LANES)

    def prepare(level):
        weights_copy(level).wait()
        hi, lo = split(weights[level])
        wide[level, :, :LANES] = hi
        wide[level, :, LANES : 2 * LANES] = hi
        wide[level, :, 2 * LANES :] = lo

    def product(index, x, first, n):
        hi, lo = split(x)
        all_kinds = dot(jnp.concatenate([hi, lo, hi], axis=1), wide[index], NT).reshape(n, V, KINDS * LANES)
        kind = jnp.concatenate(
            [jnp.broadcast_to(kinds[index, pl.ds(first + g, 1), :], (V, LANES))[None] for g in range(n)], axis=0
        )
        y = all_kinds[:, :, :LANES]
        for k in range(1, KINDS):
            y = jnp.where(kind == float(k), all_kinds[:, :, k * LANES : (k + 1) * LANES], y)
        return y

    def seven_levels(first, part, before, source):
        for i in range(7):
            before(i)
            halves = []
            for h in range(2):
                x = source(h) if i == 0 else work[part, h, i % 2]
                y = product(first + i, x.reshape(64 * V, LANES), 64 * h, 64)
                if i < 6:
                    work[part, h, (i + 1) % 2] = exchange(y)
                halves.append(y)
        return exchange(jnp.concatenate(halves, axis=0))

    order = lax.broadcasted_iota(jnp.int32, (1, 256), 1)
    order_rows = lax.broadcasted_iota(jnp.int32, (256, LANES), 0)

    def set_early_kinds(level):
        set_kinds(level, level, pattern_ref[level : level + 1, :].astype(F32), order, order_rows)

    set_early_kinds(0)
    rows = []
    for level in range(7, 15):
        row = pattern_ref[level : level + 1, :].astype(F32)
        rows += [row[:, :128], row[:, 128:]]
    rows = jnp.concatenate(rows + [jnp.zeros((128 - len(rows), 128), F32)], axis=0).astype(BF16)
    down = lax.broadcasted_iota(jnp.int32, (128, 128), 0)
    across = lax.broadcasted_iota(jnp.int32, (128, 128), 1)
    permute = jnp.where(reverse(down, 7) == across, 1.0, 0.0).astype(BF16)
    sent[0][:, V : V + 1, :] = dot(permute, rows, NT)[:, None, :]

    src_box = src_box_ref[...]
    src_row = row_of(src_box & 255, 0)
    hi, lo = split(half_masks(chebyshev(src_offset_ref[...]), src_box & 1))
    basis_in[:LANES] = hi
    basis_in[LANES:] = lo
    tgt_box = tgt_box_ref[...]
    tgt_row = (tgt_box >> 1) & 127
    hi, lo = split(half_masks(chebyshev(tgt_offset_ref[...]), tgt_box & 1))
    basis_out[:LANES] = hi
    basis_out[LANES : 2 * LANES] = hi
    basis_out[2 * LANES :] = lo

    def expand(part, half):
        hi, lo = split(values_ref[part * V : (part + 1) * V, :])
        here = src_row[None] == lax.broadcasted_iota(jnp.int32, (64, 1, 1), 0) + half * 64
        total = 0.0
        for term in (hi, lo):
            masked = jnp.where(here, term.astype(F32)[None], 0.0).reshape(64 * V, -1).astype(BF16)
            total += dot(masked, basis_in[...], NT)
        return total[:, :LANES] + total[:, LANES:]

    def evaluate(part, x):
        hi, lo = split(x)
        x = jnp.concatenate([hi, lo, hi], axis=1)
        n = tgt_row.shape[1]
        Q = 256
        for q in range(0, n, Q):
            h = dot(x, basis_out[:, q : q + Q], NN).reshape(128, V, Q)
            g = lax.broadcasted_iota(jnp.int32, (128, 1, 1), 0)
            total = jnp.sum(jnp.where(tgt_row[None, :, q : q + Q] == g, h, 0.0), axis=0)
            out_ref[part * V : (part + 1) * V, q : q + Q] = 0.125 * total

    def at_once(act):
        def turn(i):
            if i == 0:
                for peer in peers:
                    act(peer)

        return turn

    def nothing(i):
        pass

    def wait_all(ref, sem):
        ref = ref.at[pl.ds(0, devices - 1)]
        pltpu.make_async_copy(ref, ref, sem).wait()

    def up(part, before):
        @pl.loop(0, 1)
        def _(once):
            for h in range(2):
                work[part, h, 1] = expand(part, h).reshape(64, V, LANES)

        out = seven_levels(0, part, before, lambda h: work[part, h, 1])
        sent[part][:, :V, :] = out
        arrived[part][pl.ds(slot, 1)] = sent[part][pl.ds(me, 1)]

    prepare(0)

    def first_turn(i):
        prepare(i + 1)
        if i < 6:
            set_early_kinds(i + 1)

    up(0, first_turn)
    pl.semaphore_wait(barrier, devices - 1)
    for part in range(1, parts):
        up(part, at_once(lambda peer, part=part: block_copy(part - 1, peer).start()))

    wait_all(arrived[0], recv_sem.at[0])
    got = arrived[0][:, V, :].astype(BF16)
    pick = jnp.where(down == across, 1.0, 0.0).astype(BF16)
    got = dot(pick, got, NT)

    def source_box(place):
        at = place & 127
        return ((reverse(at & 63, 6) + (at & 64)) << 1) + (place >> 7)

    order, order_rows = source_box(order), source_box(order_rows)

    def late_row(level):
        return jnp.concatenate([got[2 * level : 2 * level + 1], got[2 * level + 1 : 2 * level + 2]], axis=1)

    def set_late_kinds(level):
        set_kinds(7 + level, level, late_row(level), order, order_rows)

    def fold_last_level():
        at_box = reverse(tgt_box & 255, 8)
        here = jnp.where(order_rows[:, :1] == at_box, 1.0, 0.0).astype(BF16)
        kind = dot(jnp.broadcast_to(late_row(7), (8, 256)).astype(BF16), here, NN)[:1]
        weights_copy(14).wait()
        turned = [jnp.transpose(weights[14, k * LANES : (k + 1) * LANES]) for k in range(KINDS)]
        hi, lo = split(jnp.concatenate(turned, axis=0))
        all_kinds = dot(jnp.concatenate([hi, lo, hi], axis=1), basis_out[...], NN)
        y = all_kinds[:LANES]
        for k in range(1, KINDS):
            y = jnp.where(kind == float(k), all_kinds[k * LANES : (k + 1) * LANES], y)
        hi, lo = split(y)
        basis_out[:LANES] = hi
        basis_out[LANES : 2 * LANES] = hi
        basis_out[2 * LANES :] = lo

    set_late_kinds(0)

    for part in range(parts):
        if part == 0:
            turn = at_once(lambda peer: block_copy(parts - 1, peer).start())

            def before(i):
                turn(i)
                if i < 6:
                    prepare(8 + i)
                    set_late_kinds(1 + i)
                if i == 3:
                    fold_last_level()
        else:
            wait_all(arrived[part], recv_sem.at[part])
            before = nothing
        x = seven_levels(7, part, before, lambda h: arrived[part][64 * h : 64 * h + 64, :V, :])
        evaluate(part, x.reshape(128 * V, LANES))

    for part in range(parts):
        wait_all(sent[part], send_sem.at[part])


def solution(mesh):
    src_size, tgt_size = mesh.shape["src"], mesh.shape["tgt"]
    devices = src_size * tgt_size
    parts = 2

    def on_device(src_values, src_offset, src_box, tgt_offset, tgt_box, pattern, operators):
        funcs, points = src_values.shape
        V = funcs // parts
        vmem = pl.BlockSpec(memory_space=pltpu.VMEM)
        blocks = [pltpu.VMEM((devices, V + (part == 0), LANES), F32) for part in range(parts)]
        return pl.pallas_call(
            functools.partial(kernel, V, parts, src_size, tgt_size),
            out_shape=jax.ShapeDtypeStruct((funcs, points), F32),
            in_specs=[vmem] * 6 + [pl.BlockSpec(memory_space=pl.ANY)],
            out_specs=vmem,
            scratch_shapes=[
                pltpu.VMEM((15, KINDS * LANES, LANES), F32),
                pltpu.VMEM((15, KINDS * LANES, 3 * LANES), BF16),
                pltpu.VMEM((15, 128, LANES), F32),
                pltpu.VMEM((parts, 2, 2, 64, V, LANES), F32),
                pltpu.VMEM((2 * LANES, points), BF16),
                pltpu.VMEM((3 * LANES, points), BF16),
                blocks,
                blocks,
                pltpu.SemaphoreType.DMA((15,)),
                pltpu.SemaphoreType.DMA((parts,)),
                pltpu.SemaphoreType.DMA((parts,)),
            ],
            compiler_params=pltpu.CompilerParams(
                collective_id=0, has_side_effects=True, vmem_limit_bytes=56 * 2**20
            ),
        )(
            src_values,
            src_offset.reshape(1, points),
            src_box.reshape(1, points),
            tgt_offset.reshape(1, points),
            tgt_box.reshape(1, points),
            pattern,
            operators.reshape(15, KINDS * LANES, LANES),
        )

    placed = (
        P(None, ("src", "tgt")),
        P(("src", "tgt")),
        P(("src", "tgt")),
        P(("src", "tgt")),
        P(("src", "tgt")),
        P(None, ("src", "tgt")),
        P(),
    )
    return jax.shard_map(
        on_device, mesh=mesh, in_specs=placed, out_specs=P(None, ("src", "tgt")), check_vma=False
    )
```

```python
import functools

import jax
import jax.numpy as jnp
from jax import lax
from jax.experimental import pallas as pl
from jax.experimental.pallas import tpu as pltpu
from jax.sharding import PartitionSpec as P

RANK = 64
KINDS = 4
LANES = 2 * RANK
MESH = pl.DeviceIdType.MESH
F32, BF16 = jnp.float32, jnp.bfloat16
NT = (((1,), (1,)), ((), ()))
NN = (((1,), (0,)), ((), ()))


def split(x):
    hi = x.astype(BF16)
    return hi, (x - hi.astype(F32)).astype(BF16)


def dot(a, b, dims):
    return lax.dot_general(a, b, dims, preferred_element_type=F32)


def bit(x, k):
    return (x >> k) & 1


def reverse(x, n):
    return sum(bit(x, k) << (n - 1 - k) for k in range(n))


def early_row(box, level, flip):
    if level == 0:
        return reverse(box >> 1, 7)
    parts = [bit(box, level - 1 - k if k < level - 1 else 6 + level - k) << k for k in range(6)]
    return sum(parts) + ((bit(box, 0) ^ flip) << 6)


def late_row_of(box, level):
    parts = [bit(box, level - 1 - k) << k for k in range(level)]
    parts += [bit(box, 6 + level - k) << k for k in range(level, 6)]
    return sum(parts) + (bit(box, 7) << 6)


def chebyshev(points):
    n = points.shape[1]
    x = jnp.broadcast_to(points, (8, n))
    rows = [jnp.ones_like(x), x]
    for _ in range(7):
        rows.append(2.0 * x * rows[-1] - rows[-2])
    at = lax.broadcasted_iota(jnp.int32, (8, n), 0)
    now, before = rows[0], rows[8]
    for k in range(1, 8):
        now = jnp.where(at == k, rows[k], now)
        before = jnp.where(at == k, rows[8 - k], before)
    twice = 2.0 * rows[8]
    blocks = [now]
    for _ in range(RANK // 8 - 1):
        now, before = twice * now - before, now
        blocks.append(now)
    return jnp.concatenate(blocks, axis=0)


def half_masks(basis, child):
    return jnp.concatenate([jnp.where(child == c, basis, 0.0) for c in range(2)], axis=0)


def kernel(
    V, parts, lag, src_size, tgt_size,
    values_ref, src_offset_ref, src_box_ref, tgt_offset_ref, tgt_box_ref, pattern_ref, weights_ref,
    out_ref,
    weights, wide, last, kinds, work, basis_in, basis_out, sent, arrived,
    weights_sem, send_sem, recv_sem,
):
    devices = src_size * tgt_size
    levels = weights.shape[0]
    src_me, tgt_me = lax.axis_index("src"), lax.axis_index("tgt")
    me = src_me * tgt_size + tgt_me
    low, slot = lax.rem(me, 64), (me // 64) * 64
    for k in range(6):
        slot = slot + lax.rem(low // 2**k, 2) * 2 ** (5 - k)
    src_of = [lax.rem(src_me + k, src_size) for k in range(src_size)]
    tgt_of = [lax.rem(tgt_me + k, tgt_size) for k in range(tgt_size)]
    peers = [(s, t) for s in src_of for t in tgt_of][1:]
    group = src_size // 2
    my_half = src_me // group
    flip = 1 - my_half
    in_half = [lax.rem(src_me + k, group) for k in range(group)]
    groups = [
        [(flip * group + s, t) for s in in_half for t in tgt_of],
        [(my_half * group + s, t) for s in in_half for t in tgt_of][1:],
    ]

    def weights_copy(level):
        return pltpu.make_async_copy(weights_ref.at[level], weights.at[level], weights_sem.at[level])

    for level in range(levels):
        weights_copy(level).start()

    barrier = pltpu.get_barrier_semaphore()

    def greet(peer):
        pl.semaphore_signal(barrier, inc=1, device_id=peer, device_id_type=MESH)

    for peer in peers:
        greet(peer)

    def block_copy(part, which, peer):
        row = which * 64 + lax.rem(peer[0], group) * tgt_size + peer[1]
        return pltpu.make_async_remote_copy(
            src_ref=sent[part].at[row],
            dst_ref=arrived[part].at[slot],
            send_sem=send_sem.at[part],
            recv_sem=recv_sem.at[part],
            device_id=peer,
            device_id_type=MESH,
        )

    lane_low = lax.broadcasted_iota(jnp.int32, (1, 1, LANES), 2) < RANK

    def set_kinds(index, level, values, row_in_order, order_rows):
        rows = lax.broadcasted_iota(jnp.int32, (128, 256), 0)
        picked = jnp.where(row_in_order == rows, values, 0.0).astype(BF16)
        lane_child = (lax.broadcasted_iota(jnp.int32, (256, LANES), 1) >= RANK).astype(jnp.int32)
        spread = jnp.where(bit(order_rows, level) == lane_child, 1.0, 0.0).astype(BF16)
        kinds[index] = dot(picked, spread, NN)

    def swap(y):
        n = y.shape[0]

        def turned(a):
            return pltpu.roll(a.reshape(n // 2 * V, LANES), RANK, 1).reshape(n // 2, V, LANES)

        top, low = y[: n // 2], y[n // 2 :]
        n0 = jnp.where(lane_low, top, turned(low))
        n1 = jnp.where(lane_low, turned(top), low)
        return n0, n1

    def exchange(y):
        return jnp.stack(swap(y), axis=1).reshape(y.shape[0], V, LANES)

    def prepare(level):
        weights_copy(level).wait()
        hi, lo = split(weights[level])
        wide[level, :, :LANES] = hi
        wide[level, :, LANES : 2 * LANES] = hi
        wide[level, :, 2 * LANES :] = lo

    def product(index, x, first, n):
        hi, lo = split(x)
        all_kinds = dot(jnp.concatenate([hi, lo, hi], axis=1), wide[index], NT).reshape(n, V, KINDS * LANES)
        kind = jnp.concatenate(
            [jnp.broadcast_to(kinds[index, pl.ds(first + g, 1), :], (V, LANES))[None] for g in range(n)], axis=0
        )
        y = all_kinds[:, :, :LANES]
        for k in range(1, KINDS):
            y = jnp.where(kind == float(k), all_kinds[:, :, k * LANES : (k + 1) * LANES], y)
        return y

    def on_halves(levels_here, part, before, source):
        for i, index in enumerate(levels_here):
            before(i)
            halves = []
            for h in range(2):
                y = source(h) if i == 0 else work[part, h, i % 2]
                if index is not None:
                    y = product(index, y.reshape(64 * V, LANES), 64 * h, 64)
                if i < len(levels_here) - 1:
                    work[part, h, (i + 1) % 2] = exchange(y)
                halves.append(y)
        return exchange(jnp.concatenate(halves, axis=0))

    order = lax.broadcasted_iota(jnp.int32, (1, 256), 1)
    order_rows = lax.broadcasted_iota(jnp.int32, (256, LANES), 0)
    down = lax.broadcasted_iota(jnp.int32, (128, 128), 0)
    across = lax.broadcasted_iota(jnp.int32, (128, 128), 1)

    def set_early_kinds(level):
        values = pattern_ref[level : level + 1, :].astype(F32)
        set_kinds(level, level, values, early_row(order, level, flip), order_rows)

    def set_pattern_row():
        rows = []
        for level in range(7, 15):
            row = pattern_ref[level : level + 1, :].astype(F32)
            rows += [row[:, :128], row[:, 128:]]
        rows = jnp.concatenate(rows + [jnp.zeros((128 - len(rows), 128), F32)], axis=0).astype(BF16)
        permute = jnp.where(reverse(down ^ (flip << 6), 7) == across, 1.0, 0.0).astype(BF16)
        sent[0][:, V : V + 1, :] = dot(permute, rows, NT)[:, None, :]

    src_box = src_box_ref[...]
    src_row = early_row(src_box & 255, 0, flip)
    hi, lo = split(half_masks(chebyshev(src_offset_ref[...]), src_box & 1))
    basis_in[:LANES] = hi
    basis_in[LANES:] = lo
    tgt_box = tgt_box_ref[...]
    tgt_row = (tgt_box >> 1) & 127

    def set_basis_out(z):
        hi, lo = split(z)
        basis_out[:LANES] = hi
        basis_out[LANES : 2 * LANES] = hi
        basis_out[2 * LANES :] = lo

    def target_basis():
        set_basis_out(half_masks(chebyshev(tgt_offset_ref[...]), tgt_box & 1))

    def expand(part, half):
        hi, lo = split(values_ref[part * V : (part + 1) * V, :])
        here = src_row[None] == lax.broadcasted_iota(jnp.int32, (64, 1, 1), 0) + half * 64
        total = 0.0
        for term in (hi, lo):
            masked = jnp.where(here, term.astype(F32)[None], 0.0).reshape(64 * V, -1).astype(BF16)
            total += dot(masked, basis_in[...], NT)
        return total[:, :LANES] + total[:, LANES:]

    def evaluate(part, x):
        hi, lo = split(x)
        x = jnp.concatenate([hi, lo, hi], axis=1)
        n = tgt_row.shape[1]
        Q = 256
        for q in range(0, n, Q):
            h = dot(x, basis_out[:, q : q + Q], NN).reshape(128, V, Q)
            g = lax.broadcasted_iota(jnp.int32, (128, 1, 1), 0)
            total = jnp.sum(jnp.where(tgt_row[None, :, q : q + Q] == g, h, 0.0), axis=0)
            out_ref[part * V : (part + 1) * V, q : q + Q] = 0.125 * total

    def nothing(i):
        pass

    def wait_all(ref, sem):
        ref = ref.at[pl.ds(0, devices - 1)]
        pltpu.make_async_copy(ref, ref, sem).wait()

    def up(part, before):
        @pl.loop(0, 1)
        def _(once):
            for h in range(2):
                work[part, h, 1] = expand(part, h).reshape(64, V, LANES)

        before(0)
        y = [product(0, work[part, h, 1].reshape(64 * V, LANES), 64 * h, 64) for h in range(2)]
        zero, one = swap(jnp.concatenate(y, axis=0))
        work[part, 0, 0] = jnp.where(flip == 1, one, zero)
        work[part, 1, 0] = jnp.where(flip == 1, zero, one)
        for step in range(1, 8 + lag):
            before(step)
            for which in range(2):
                level = step - lag * which
                if not 1 <= level <= 7:
                    continue
                y = product(level, work[part, which, (level - 1) % 2].reshape(64 * V, LANES), 64 * which, 64)
                if level < 7:
                    work[part, which, level % 2] = exchange(y)
                else:
                    sent[part][64 * which : 64 * which + 64, :V, :] = y

        arrived[part][pl.ds(slot, 1)] = sent[part][pl.ds(64 + lax.rem(me, 64), 1)]

    def send(part, which):
        for peer in groups[which]:
            block_copy(part, which, peer).start()

    def apply_last_weights():
        weights_copy(14).wait()
        turned = [jnp.transpose(weights[14, k * LANES : (k + 1) * LANES]) for k in range(KINDS)]
        hi, lo = split(jnp.concatenate(turned, axis=0))
        last[...] = dot(jnp.concatenate([hi, lo, hi], axis=1), basis_out[...], NN)

    set_early_kinds(0)
    prepare(0)

    def beside_first(i):
        if i < 7:
            prepare(i + 1)
            set_early_kinds(i + 1)
        if i == 2:
            set_pattern_row()
        if i == 8:
            pl.semaphore_wait(barrier, devices - 1)
            send(0, 0)

    up(0, beside_first)
    if lag == 0:
        pl.semaphore_wait(barrier, devices - 1)
        send(0, 0)

    def beside_second(i):
        if i == 0:
            send(0, 1)
        elif i < 7:
            prepare(7 + i)
        if i == 1:
            target_basis()
        if i == 4:
            apply_last_weights()
        if i == 8:
            send(1, 0)

    up(1, beside_second)
    if lag == 0:
        send(1, 0)
    send(1, 1)

    wait_all(arrived[0], recv_sem.at[0])
    got = arrived[0][:, V, :].astype(BF16)
    pick = jnp.where(down == across, 1.0, 0.0).astype(BF16)
    got = dot(pick, got, NT)

    def source_box(place):
        at = place & 127
        return ((reverse(at & 63, 6) + (at & 64)) << 1) + (place >> 7)

    late_order, late_order_rows = source_box(order), source_box(order_rows)

    def late_row(level):
        return jnp.concatenate([got[2 * level : 2 * level + 1], got[2 * level + 1 : 2 * level + 2]], axis=1)

    def set_late_kinds(level):
        set_kinds(7 + level, level, late_row(level), late_row_of(late_order, level), late_order_rows)

    def pick_last_kind():
        at_box = reverse(tgt_box & 255, 8)
        here = jnp.where(late_order_rows[:, :1] == at_box, 1.0, 0.0).astype(BF16)
        kind = dot(jnp.broadcast_to(late_row(7), (8, 256)).astype(BF16), here, NN)[:1]
        z = last[:LANES]
        for k in range(1, KINDS):
            z = jnp.where(kind == float(k), last[k * LANES : (k + 1) * LANES], z)
        set_basis_out(z)

    def beside_third(i):
        if i < 6:
            set_late_kinds(1 + i)
        if i == 4:
            pick_last_kind()

    for part in range(parts):
        if part > 0:
            wait_all(arrived[part], recv_sem.at[part])
        x = on_halves(
            [None] + list(range(8, 14)),
            part,
            nothing if part else beside_third,
            lambda h: arrived[part][64 * h : 64 * h + 64, :V, :],
        )
        evaluate(part, x.reshape(128 * V, LANES))

    for part in range(parts):
        wait_all(sent[part], send_sem.at[part])


def solution(mesh):
    src_size, tgt_size = mesh.shape["src"], mesh.shape["tgt"]
    devices = src_size * tgt_size
    parts, lag = 2, 3

    def on_device(src_values, src_offset, src_box, tgt_offset, tgt_box, pattern, operators):
        funcs, points = src_values.shape
        V = funcs // parts
        vmem = pl.BlockSpec(memory_space=pltpu.VMEM)
        blocks = [pltpu.VMEM((devices, V + (part == 0), LANES), F32) for part in range(parts)]
        return pl.pallas_call(
            functools.partial(kernel, V, parts, lag, src_size, tgt_size),
            out_shape=jax.ShapeDtypeStruct((funcs, points), F32),
            in_specs=[vmem] * 6 + [pl.BlockSpec(memory_space=pl.ANY)],
            out_specs=vmem,
            scratch_shapes=[
                pltpu.VMEM((15, KINDS * LANES, LANES), F32),
                pltpu.VMEM((15, KINDS * LANES, 3 * LANES), BF16),
                pltpu.VMEM((KINDS * LANES, points), F32),
                pltpu.VMEM((15, 128, LANES), F32),
                pltpu.VMEM((parts, 2, 2, 64, V, LANES), F32),
                pltpu.VMEM((2 * LANES, points), BF16),
                pltpu.VMEM((3 * LANES, points), BF16),
                blocks,
                blocks,
                pltpu.SemaphoreType.DMA((15,)),
                pltpu.SemaphoreType.DMA((parts,)),
                pltpu.SemaphoreType.DMA((parts,)),
            ],
            compiler_params=pltpu.CompilerParams(
                collective_id=0, has_side_effects=True, vmem_limit_bytes=56 * 2**20
            ),
        )(
            src_values,
            src_offset.reshape(1, points),
            src_box.reshape(1, points),
            tgt_offset.reshape(1, points),
            tgt_box.reshape(1, points),
            pattern,
            operators.reshape(15, KINDS * LANES, LANES),
        )

    placed = (
        P(None, ("src", "tgt")),
        P(("src", "tgt")),
        P(("src", "tgt")),
        P(("src", "tgt")),
        P(("src", "tgt")),
        P(None, ("src", "tgt")),
        P(),
    )
    return jax.shard_map(
        on_device, mesh=mesh, in_specs=placed, out_specs=P(None, ("src", "tgt")), check_vma=False
    )
```

```python
import functools

import jax
import jax.numpy as jnp
from jax import lax
from jax.experimental import pallas as pl
from jax.experimental.pallas import tpu as pltpu
from jax.sharding import PartitionSpec as P

RANK = 64
KINDS = 4
LANES = 2 * RANK
MESH = pl.DeviceIdType.MESH
F32, BF16 = jnp.float32, jnp.bfloat16
NT = (((1,), (1,)), ((), ()))
NN = (((1,), (0,)), ((), ()))


def split(x):
    hi = x.astype(BF16)
    return hi, (x - hi.astype(F32)).astype(BF16)


def dot(a, b, dims):
    return lax.dot_general(a, b, dims, preferred_element_type=F32)


def bit(x, k):
    return (x >> k) & 1


def reverse(x, n):
    return sum(bit(x, k) << (n - 1 - k) for k in range(n))


def early_row(box, level, flip):
    if level == 0:
        return reverse(box >> 1, 7)
    parts = [bit(box, level - 1 - k if k < level - 1 else 6 + level - k) << k for k in range(6)]
    return sum(parts) + ((bit(box, 0) ^ flip) << 6)


def late_row_of(box, level):
    parts = [bit(box, level - 1 - k) << k for k in range(level)]
    parts += [bit(box, 6 + level - k) << k for k in range(level, 6)]
    return sum(parts) + (bit(box, 7) << 6)


def chebyshev(points):
    n = points.shape[1]
    x = jnp.broadcast_to(points, (8, n))
    rows = [jnp.ones_like(x), x]
    for _ in range(7):
        rows.append(2.0 * x * rows[-1] - rows[-2])
    at = lax.broadcasted_iota(jnp.int32, (8, n), 0)
    now, before = rows[0], rows[8]
    for k in range(1, 8):
        now = jnp.where(at == k, rows[k], now)
        before = jnp.where(at == k, rows[8 - k], before)
    twice = 2.0 * rows[8]
    blocks = [now]
    for _ in range(RANK // 8 - 1):
        now, before = twice * now - before, now
        blocks.append(now)
    return jnp.concatenate(blocks, axis=0)


def half_masks(basis, child):
    return jnp.concatenate([jnp.where(child == c, basis, 0.0) for c in range(2)], axis=0)


def kernel(
    V, parts, lag, src_size, tgt_size,
    values_ref, src_offset_ref, src_box_ref, tgt_offset_ref, tgt_box_ref, pattern_ref, weights_ref,
    out_ref,
    weights, wide, last, kinds, work, basis_in, basis_out, sent, arrived,
    weights_sem, send_sem, recv_sem,
):
    devices = src_size * tgt_size
    levels = weights.shape[0]
    src_me, tgt_me = lax.axis_index("src"), lax.axis_index("tgt")
    me = src_me * tgt_size + tgt_me
    low, slot = lax.rem(me, 64), (me // 64) * 64
    for k in range(6):
        slot = slot + lax.rem(low // 2**k, 2) * 2 ** (5 - k)
    src_of = [lax.rem(src_me + k, src_size) for k in range(src_size)]
    tgt_of = [lax.rem(tgt_me + k, tgt_size) for k in range(tgt_size)]
    peers = [(s, t) for s in src_of for t in tgt_of][1:]
    group = src_size // 2
    my_half = src_me // group
    flip = 1 - my_half
    in_half = [lax.rem(src_me + k, group) for k in range(group)]
    groups = [
        [(flip * group + s, t) for s in in_half for t in tgt_of],
        [(my_half * group + s, t) for s in in_half for t in tgt_of][1:],
    ]

    def weights_copy(level):
        return pltpu.make_async_copy(weights_ref.at[level], weights.at[level], weights_sem.at[level])

    for level in range(levels):
        weights_copy(level).start()

    barrier = pltpu.get_barrier_semaphore()

    def greet(peer):
        pl.semaphore_signal(barrier, inc=1, device_id=peer, device_id_type=MESH)

    for peer in peers:
        greet(peer)

    def block_copy(part, which, peer):
        row = which * 64 + lax.rem(peer[0], group) * tgt_size + peer[1]
        return pltpu.make_async_remote_copy(
            src_ref=sent[part].at[row],
            dst_ref=arrived[part].at[slot],
            send_sem=send_sem.at[part],
            recv_sem=recv_sem.at[part],
            device_id=peer,
            device_id_type=MESH,
        )

    lane_low = lax.broadcasted_iota(jnp.int32, (1, 1, LANES), 2) < RANK

    def set_kinds(index, level, values, row_in_order, order_rows):
        rows = lax.broadcasted_iota(jnp.int32, (128, 256), 0)
        picked = jnp.where(row_in_order == rows, values, 0.0).astype(BF16)
        lane_child = (lax.broadcasted_iota(jnp.int32, (256, LANES), 1) >= RANK).astype(jnp.int32)
        spread = jnp.where(bit(order_rows, level) == lane_child, 1.0, 0.0).astype(BF16)
        kinds[index] = dot(picked, spread, NN)

    def swap(y):
        n = y.shape[0]

        def turned(a):
            return pltpu.roll(a.reshape(n // 2 * V, LANES), RANK, 1).reshape(n // 2, V, LANES)

        top, low = y[: n // 2], y[n // 2 :]
        n0 = jnp.where(lane_low, top, turned(low))
        n1 = jnp.where(lane_low, turned(top), low)
        return n0, n1

    def exchange(y):
        return jnp.stack(swap(y), axis=1).reshape(y.shape[0], V, LANES)

    def prepare(level):
        weights_copy(level).wait()
        hi, lo = split(weights[level])
        wide[level, :, :LANES] = hi
        wide[level, :, LANES : 2 * LANES] = hi
        wide[level, :, 2 * LANES :] = lo

    def product(index, x, first, n):
        hi, lo = split(x)
        all_kinds = dot(jnp.concatenate([hi, lo, hi], axis=1), wide[index], NT).reshape(n, V, KINDS * LANES)
        kind = jnp.concatenate(
            [jnp.broadcast_to(kinds[index, pl.ds(first + g, 1), :], (V, LANES))[None] for g in range(n)], axis=0
        )
        y = all_kinds[:, :, :LANES]
        for k in range(1, KINDS):
            y = jnp.where(kind == float(k), all_kinds[:, :, k * LANES : (k + 1) * LANES], y)
        return y

    def on_halves(levels_here, part, before, source):
        for i, index in enumerate(levels_here):
            before(i)
            halves = []
            for h in range(2):
                y = source(h) if i == 0 else work[part, h, i % 2]
                if index is not None:
                    y = product(index, y.reshape(64 * V, LANES), 64 * h, 64)
                if i < len(levels_here) - 1:
                    work[part, h, (i + 1) % 2] = exchange(y)
                halves.append(y)
        return exchange(jnp.concatenate(halves, axis=0))

    order = lax.broadcasted_iota(jnp.int32, (1, 256), 1)
    order_rows = lax.broadcasted_iota(jnp.int32, (256, LANES), 0)
    down = lax.broadcasted_iota(jnp.int32, (128, 128), 0)
    across = lax.broadcasted_iota(jnp.int32, (128, 128), 1)

    def set_early_kinds(level):
        values = pattern_ref[level : level + 1, :].astype(F32)
        set_kinds(level, level, values, early_row(order, level, flip), order_rows)

    def set_pattern_row():
        rows = []
        for level in range(7, 15):
            row = pattern_ref[level : level + 1, :].astype(F32)
            rows += [row[:, :128], row[:, 128:]]
        rows = jnp.concatenate(rows + [jnp.zeros((128 - len(rows), 128), F32)], axis=0).astype(BF16)
        permute = jnp.where(reverse(down ^ (flip << 6), 7) == across, 1.0, 0.0).astype(BF16)
        sent[0][:, V : V + 1, :] = dot(permute, rows, NT)[:, None, :]

    src_box = src_box_ref[...]
    src_row = early_row(src_box & 255, 0, flip)
    hi, lo = split(half_masks(chebyshev(src_offset_ref[...]), src_box & 1))
    basis_in[:LANES] = hi
    basis_in[LANES:] = lo
    tgt_box = tgt_box_ref[...]
    tgt_row = (tgt_box >> 1) & 127

    def set_basis_out(z):
        hi, lo = split(z)
        basis_out[:LANES] = hi
        basis_out[LANES : 2 * LANES] = hi
        basis_out[2 * LANES :] = lo

    def target_basis():
        set_basis_out(half_masks(chebyshev(tgt_offset_ref[...]), tgt_box & 1))

    def expand(part, half):
        hi, lo = split(values_ref[part * V : (part + 1) * V, :])
        here = src_row[None] == lax.broadcasted_iota(jnp.int32, (64, 1, 1), 0) + half * 64
        total = 0.0
        for term in (hi, lo):
            masked = jnp.where(here, term.astype(F32)[None], 0.0).reshape(64 * V, -1).astype(BF16)
            total += dot(masked, basis_in[...], NT)
        return total[:, :LANES] + total[:, LANES:]

    def evaluate(part, x):
        hi, lo = split(x)
        x = jnp.concatenate([hi, lo, hi], axis=1)
        n = tgt_row.shape[1]
        Q = 256
        for q in range(0, n, Q):
            h = dot(x, basis_out[:, q : q + Q], NN).reshape(128, V, Q)
            g = lax.broadcasted_iota(jnp.int32, (128, 1, 1), 0)
            total = jnp.sum(jnp.where(tgt_row[None, :, q : q + Q] == g, h, 0.0), axis=0)
            out_ref[part * V : (part + 1) * V, q : q + Q] = 0.125 * total

    def nothing(i):
        pass

    def wait_all(ref, sem):
        ref = ref.at[pl.ds(0, devices - 1)]
        pltpu.make_async_copy(ref, ref, sem).wait()

    def up(part, before):
        @pl.loop(0, 1)
        def _(once):
            for h in range(2):
                work[part, h, 1] = expand(part, h).reshape(64, V, LANES)

        before(0)
        y = [product(0, work[part, h, 1].reshape(64 * V, LANES), 64 * h, 64) for h in range(2)]
        zero, one = swap(jnp.concatenate(y, axis=0))
        work[part, 0, 0] = jnp.where(flip == 1, one, zero)
        work[part, 1, 0] = jnp.where(flip == 1, zero, one)
        for step in range(1, 8 + lag):
            before(step)
            for which in range(2):
                level = step - lag * which
                if not 1 <= level <= 7:
                    continue
                y = product(level, work[part, which, (level - 1) % 2].reshape(64 * V, LANES), 64 * which, 64)
                if level < 7:
                    work[part, which, level % 2] = exchange(y)
                else:
                    sent[part][64 * which : 64 * which + 64, :V, :] = y

        arrived[part][pl.ds(slot, 1)] = sent[part][pl.ds(64 + lax.rem(me, 64), 1)]

    def send(part, which):
        for peer in groups[which]:
            block_copy(part, which, peer).start()

    def apply_last_weights():
        weights_copy(14).wait()
        turned = [jnp.transpose(weights[14, k * LANES : (k + 1) * LANES]) for k in range(KINDS)]
        hi, lo = split(jnp.concatenate(turned, axis=0))
        last[...] = dot(jnp.concatenate([hi, lo, hi], axis=1), basis_out[...], NN)

    set_early_kinds(0)
    prepare(0)

    def beside_first(i):
        if i < 7:
            prepare(i + 1)
            set_early_kinds(i + 1)
        if i == 2:
            set_pattern_row()
        if i == 8:
            pl.semaphore_wait(barrier, devices - 1)
            send(0, 0)

    up(0, beside_first)
    if lag == 0:
        pl.semaphore_wait(barrier, devices - 1)
        send(0, 0)

    def beside_second(i):
        if i == 0:
            send(0, 1)
        if i == 8:
            send(1, 0)

    up(1, beside_second)
    if lag == 0:
        send(1, 0)
    send(1, 1)
    target_basis()
    apply_last_weights()
    for level in range(8, 14):
        prepare(level)

    wait_all(arrived[0], recv_sem.at[0])
    got = arrived[0][:, V, :].astype(BF16)
    pick = jnp.where(down == across, 1.0, 0.0).astype(BF16)
    got = dot(pick, got, NT)

    def source_box(place):
        at = place & 127
        return ((reverse(at & 63, 6) + (at & 64)) << 1) + (place >> 7)

    late_order, late_order_rows = source_box(order), source_box(order_rows)

    def late_row(level):
        return jnp.concatenate([got[2 * level : 2 * level + 1], got[2 * level + 1 : 2 * level + 2]], axis=1)

    def set_late_kinds(level):
        set_kinds(7 + level, level, late_row(level), late_row_of(late_order, level), late_order_rows)

    def pick_last_kind():
        at_box = reverse(tgt_box & 255, 8)
        here = jnp.where(late_order_rows[:, :1] == at_box, 1.0, 0.0).astype(BF16)
        kind = dot(jnp.broadcast_to(late_row(7), (8, 256)).astype(BF16), here, NN)[:1]
        z = last[:LANES]
        for k in range(1, KINDS):
            z = jnp.where(kind == float(k), last[k * LANES : (k + 1) * LANES], z)
        set_basis_out(z)

    def beside_third(i):
        if i < 6:
            set_late_kinds(1 + i)
        if i == 4:
            pick_last_kind()

    for part in range(parts):
        if part > 0:
            wait_all(arrived[part], recv_sem.at[part])
        x = on_halves(
            [None] + list(range(8, 14)),
            part,
            nothing if part else beside_third,
            lambda h: arrived[part][64 * h : 64 * h + 64, :V, :],
        )
        evaluate(part, x.reshape(128 * V, LANES))

    for part in range(parts):
        wait_all(sent[part], send_sem.at[part])


def solution(mesh):
    src_size, tgt_size = mesh.shape["src"], mesh.shape["tgt"]
    devices = src_size * tgt_size
    parts, lag = 2, 3

    def on_device(src_values, src_offset, src_box, tgt_offset, tgt_box, pattern, operators):
        funcs, points = src_values.shape
        V = funcs // parts
        vmem = pl.BlockSpec(memory_space=pltpu.VMEM)
        blocks = [pltpu.VMEM((devices, V + (part == 0), LANES), F32) for part in range(parts)]
        return pl.pallas_call(
            functools.partial(kernel, V, parts, lag, src_size, tgt_size),
            out_shape=jax.ShapeDtypeStruct((funcs, points), F32),
            in_specs=[vmem] * 6 + [pl.BlockSpec(memory_space=pl.ANY)],
            out_specs=vmem,
            scratch_shapes=[
                pltpu.VMEM((15, KINDS * LANES, LANES), F32),
                pltpu.VMEM((15, KINDS * LANES, 3 * LANES), BF16),
                pltpu.VMEM((KINDS * LANES, points), F32),
                pltpu.VMEM((15, 128, LANES), F32),
                pltpu.VMEM((parts, 2, 2, 64, V, LANES), F32),
                pltpu.VMEM((2 * LANES, points), BF16),
                pltpu.VMEM((3 * LANES, points), BF16),
                blocks,
                blocks,
                pltpu.SemaphoreType.DMA((15,)),
                pltpu.SemaphoreType.DMA((parts,)),
                pltpu.SemaphoreType.DMA((parts,)),
            ],
            compiler_params=pltpu.CompilerParams(
                collective_id=0, has_side_effects=True, vmem_limit_bytes=56 * 2**20
            ),
        )(
            src_values,
            src_offset.reshape(1, points),
            src_box.reshape(1, points),
            tgt_offset.reshape(1, points),
            tgt_box.reshape(1, points),
            pattern,
            operators.reshape(15, KINDS * LANES, LANES),
        )

    placed = (
        P(None, ("src", "tgt")),
        P(("src", "tgt")),
        P(("src", "tgt")),
        P(("src", "tgt")),
        P(("src", "tgt")),
        P(None, ("src", "tgt")),
        P(),
    )
    return jax.shard_map(
        on_device, mesh=mesh, in_specs=placed, out_specs=P(None, ("src", "tgt")), check_vma=False
    )
```

```python
import functools

import jax
import jax.numpy as jnp
from jax import lax
from jax.experimental import pallas as pl
from jax.experimental.pallas import tpu as pltpu
from jax.sharding import PartitionSpec as P

RANK = 64
KINDS = 4
LANES = 2 * RANK
MESH = pl.DeviceIdType.MESH
F32, BF16 = jnp.float32, jnp.bfloat16
NT = (((1,), (1,)), ((), ()))
NN = (((1,), (0,)), ((), ()))


def split(x):
    hi = x.astype(BF16)
    return hi, (x - hi.astype(F32)).astype(BF16)


def dot(a, b, dims):
    return lax.dot_general(a, b, dims, preferred_element_type=F32)


def bit(x, k):
    return (x >> k) & 1


def reverse(x, n):
    return sum(bit(x, k) << (n - 1 - k) for k in range(n))


def early_row(box, level, flip):
    if level == 0:
        return reverse(box >> 1, 7)
    parts = [bit(box, level - 1 - k if k < level - 1 else 6 + level - k) << k for k in range(6)]
    return sum(parts) + ((bit(box, 0) ^ flip) << 6)


def late_row_of(box, level):
    parts = [bit(box, level - 1 - k) << k for k in range(level)]
    parts += [bit(box, 6 + level - k) << k for k in range(level, 6)]
    return sum(parts) + (bit(box, 7) << 6)


def chebyshev(points):
    n = points.shape[1]
    x = jnp.broadcast_to(points, (8, n))
    rows = [jnp.ones_like(x), x]
    for _ in range(7):
        rows.append(2.0 * x * rows[-1] - rows[-2])
    at = lax.broadcasted_iota(jnp.int32, (8, n), 0)
    now, before = rows[0], rows[8]
    for k in range(1, 8):
        now = jnp.where(at == k, rows[k], now)
        before = jnp.where(at == k, rows[8 - k], before)
    twice = 2.0 * rows[8]
    blocks = [now]
    for _ in range(RANK // 8 - 1):
        now, before = twice * now - before, now
        blocks.append(now)
    return jnp.concatenate(blocks, axis=0)


def half_masks(basis, child):
    return jnp.concatenate([jnp.where(child == c, basis, 0.0) for c in range(2)], axis=0)


def kernel(
    V, parts, lag, src_size, tgt_size,
    values_ref, src_offset_ref, src_box_ref, tgt_offset_ref, tgt_box_ref, pattern_ref, weights_ref,
    out_ref,
    weights, wide, last, kinds, work, basis_in, basis_out, sent, arrived,
    weights_sem, send_sem, recv_sem,
):
    devices = src_size * tgt_size
    levels = weights.shape[0]
    src_me, tgt_me = lax.axis_index("src"), lax.axis_index("tgt")
    me = src_me * tgt_size + tgt_me
    low, slot = lax.rem(me, 64), (me // 64) * 64
    for k in range(6):
        slot = slot + lax.rem(low // 2**k, 2) * 2 ** (5 - k)
    src_of = [lax.rem(src_me + k, src_size) for k in range(src_size)]
    tgt_of = [lax.rem(tgt_me + k, tgt_size) for k in range(tgt_size)]
    peers = [(s, t) for s in src_of for t in tgt_of][1:]
    group = src_size // 2
    my_half = src_me // group
    flip = 1 - my_half
    in_half = [lax.rem(src_me + k, group) for k in range(group)]
    groups = [
        [(flip * group + s, t) for s in in_half for t in tgt_of],
        [(my_half * group + s, t) for s in in_half for t in tgt_of][1:],
    ]

    def weights_copy(level):
        return pltpu.make_async_copy(weights_ref.at[level], weights.at[level], weights_sem.at[level])

    for level in range(levels):
        weights_copy(level).start()

    barrier = pltpu.get_barrier_semaphore()

    def greet(peer):
        pl.semaphore_signal(barrier, inc=1, device_id=peer, device_id_type=MESH)

    for peer in peers:
        greet(peer)

    def block_copy(part, which, peer):
        row = which * 64 + lax.rem(peer[0], group) * tgt_size + peer[1]
        return pltpu.make_async_remote_copy(
            src_ref=sent[part].at[row],
            dst_ref=arrived[part].at[slot],
            send_sem=send_sem.at[part],
            recv_sem=recv_sem.at[part],
            device_id=peer,
            device_id_type=MESH,
        )

    lane_low = lax.broadcasted_iota(jnp.int32, (1, 1, LANES), 2) < RANK

    def set_kinds(index, level, values, row_in_order, order_rows):
        rows = lax.broadcasted_iota(jnp.int32, (128, 256), 0)
        picked = jnp.where(row_in_order == rows, values, 0.0).astype(BF16)
        lane_child = (lax.broadcasted_iota(jnp.int32, (256, LANES), 1) >= RANK).astype(jnp.int32)
        spread = jnp.where(bit(order_rows, level) == lane_child, 1.0, 0.0).astype(BF16)
        kinds[index] = dot(picked, spread, NN)

    def swap(y):
        n = y.shape[0]

        def turned(a):
            return pltpu.roll(a.reshape(n // 2 * V, LANES), RANK, 1).reshape(n // 2, V, LANES)

        top, low = y[: n // 2], y[n // 2 :]
        n0 = jnp.where(lane_low, top, turned(low))
        n1 = jnp.where(lane_low, turned(top), low)
        return n0, n1

    def exchange(y):
        return jnp.stack(swap(y), axis=1).reshape(y.shape[0], V, LANES)

    def prepare(level):
        weights_copy(level).wait()
        hi, lo = split(weights[level])
        wide[level, :, :LANES] = hi
        wide[level, :, LANES : 2 * LANES] = hi
        wide[level, :, 2 * LANES :] = lo

    def product(index, x, first, n):
        hi, lo = split(x)
        all_kinds = dot(jnp.concatenate([hi, lo, hi], axis=1), wide[index], NT).reshape(n, V, KINDS * LANES)
        kind = jnp.concatenate(
            [jnp.broadcast_to(kinds[index, pl.ds(first + g, 1), :], (V, LANES))[None] for g in range(n)], axis=0
        )
        y = all_kinds[:, :, :LANES]
        for k in range(1, KINDS):
            y = jnp.where(kind == float(k), all_kinds[:, :, k * LANES : (k + 1) * LANES], y)
        return y

    def on_halves(levels_here, part, before, source):
        for i, index in enumerate(levels_here):
            before(i)
            halves = []
            for h in range(2):
                y = source(h) if i == 0 else work[part, h, i % 2]
                if index is not None:
                    y = product(index, y.reshape(64 * V, LANES), 64 * h, 64)
                if i < len(levels_here) - 1:
                    work[part, h, (i + 1) % 2] = exchange(y)
                halves.append(y)
        return exchange(jnp.concatenate(halves, axis=0))

    order = lax.broadcasted_iota(jnp.int32, (1, 256), 1)
    order_rows = lax.broadcasted_iota(jnp.int32, (256, LANES), 0)
    down = lax.broadcasted_iota(jnp.int32, (128, 128), 0)
    across = lax.broadcasted_iota(jnp.int32, (128, 128), 1)

    def set_early_kinds(level):
        values = pattern_ref[level : level + 1, :].astype(F32)
        set_kinds(level, level, values, early_row(order, level, flip), order_rows)

    def set_pattern_row():
        rows = []
        for level in range(7, 15):
            row = pattern_ref[level : level + 1, :].astype(F32)
            rows += [row[:, :128], row[:, 128:]]
        rows = jnp.concatenate(rows + [jnp.zeros((128 - len(rows), 128), F32)], axis=0).astype(BF16)
        permute = jnp.where(reverse(down ^ (flip << 6), 7) == across, 1.0, 0.0).astype(BF16)
        sent[0][:, V : V + 1, :] = dot(permute, rows, NT)[:, None, :]

    src_box = src_box_ref[...]
    src_row = early_row(src_box & 255, 0, flip)
    hi, lo = split(half_masks(chebyshev(src_offset_ref[...]), src_box & 1))
    basis_in[:LANES] = hi
    basis_in[LANES:] = lo
    tgt_box = tgt_box_ref[...]
    tgt_row = (tgt_box >> 1) & 127

    def set_basis_out(z):
        hi, lo = split(z)
        basis_out[:LANES] = hi
        basis_out[LANES : 2 * LANES] = hi
        basis_out[2 * LANES :] = lo

    def target_basis():
        set_basis_out(half_masks(chebyshev(tgt_offset_ref[...]), tgt_box & 1))

    def expand(part, half):
        hi, lo = split(values_ref[part * V : (part + 1) * V, :])
        here = src_row[None] == lax.broadcasted_iota(jnp.int32, (64, 1, 1), 0) + half * 64
        total = 0.0
        for term in (hi, lo):
            masked = jnp.where(here, term.astype(F32)[None], 0.0).reshape(64 * V, -1).astype(BF16)
            total += dot(masked, basis_in[...], NT)
        return total[:, :LANES] + total[:, LANES:]

    def evaluate(part, x):
        hi, lo = split(x)
        x = jnp.concatenate([hi, lo, hi], axis=1)
        n = tgt_row.shape[1]
        Q = 512
        for q in range(0, n, Q):
            h = dot(x, basis_out[:, q : q + Q], NN).reshape(128, V, Q)
            g = lax.broadcasted_iota(jnp.int32, (128, 1, 1), 0)
            total = jnp.sum(jnp.where(tgt_row[None, :, q : q + Q] == g, h, 0.0), axis=0)
            out_ref[part * V : (part + 1) * V, q : q + Q] = 0.125 * total

    def nothing(i):
        pass

    def wait_all(ref, sem):
        ref = ref.at[pl.ds(0, devices - 1)]
        pltpu.make_async_copy(ref, ref, sem).wait()

    def up(part, before):
        for h in range(2):
            work[part, h, 1] = expand(part, h).reshape(64, V, LANES)

        before(0)
        y = [product(0, work[part, h, 1].reshape(64 * V, LANES), 64 * h, 64) for h in range(2)]
        zero, one = swap(jnp.concatenate(y, axis=0))
        work[part, 0, 0] = jnp.where(flip == 1, one, zero)
        work[part, 1, 0] = jnp.where(flip == 1, zero, one)
        for step in range(1, 8 + lag):
            before(step)
            for which in range(2):
                level = step - lag * which
                if not 1 <= level <= 7:
                    continue
                y = product(level, work[part, which, (level - 1) % 2].reshape(64 * V, LANES), 64 * which, 64)
                if level < 7:
                    work[part, which, level % 2] = exchange(y)
                else:
                    sent[part][64 * which : 64 * which + 64, :V, :] = y

        arrived[part][pl.ds(slot, 1)] = sent[part][pl.ds(64 + lax.rem(me, 64), 1)]

    def send(part, which):
        for peer in groups[which]:
            block_copy(part, which, peer).start()

    def apply_last_weights():
        weights_copy(14).wait()
        turned = [jnp.transpose(weights[14, k * LANES : (k + 1) * LANES]) for k in range(KINDS)]
        hi, lo = split(jnp.concatenate(turned, axis=0))
        last[...] = dot(jnp.concatenate([hi, lo, hi], axis=1), basis_out[...], NN)

    set_early_kinds(0)
    prepare(0)

    def beside_first(i):
        if i < 7:
            prepare(i + 1)
            set_early_kinds(i + 1)
        if i == 2:
            set_pattern_row()
        if i == 8:
            pl.semaphore_wait(barrier, devices - 1)
            send(0, 0)

    up(0, beside_first)
    if lag == 0:
        pl.semaphore_wait(barrier, devices - 1)
        send(0, 0)

    def beside_second(i):
        if i == 0:
            send(0, 1)
        if i == 8:
            send(1, 0)

    up(1, beside_second)
    if lag == 0:
        send(1, 0)
    send(1, 1)
    target_basis()
    apply_last_weights()
    for level in range(8, 14):
        prepare(level)

    wait_all(arrived[0], recv_sem.at[0])
    got = arrived[0][:, V, :].astype(BF16)
    pick = jnp.where(down == across, 1.0, 0.0).astype(BF16)
    got = dot(pick, got, NT)

    def source_box(place):
        at = place & 127
        return ((reverse(at & 63, 6) + (at & 64)) << 1) + (place >> 7)

    late_order, late_order_rows = source_box(order), source_box(order_rows)

    def late_row(level):
        return jnp.concatenate([got[2 * level : 2 * level + 1], got[2 * level + 1 : 2 * level + 2]], axis=1)

    def set_late_kinds(level):
        set_kinds(7 + level, level, late_row(level), late_row_of(late_order, level), late_order_rows)

    def pick_last_kind():
        at_box = reverse(tgt_box & 255, 8)
        here = jnp.where(late_order_rows[:, :1] == at_box, 1.0, 0.0).astype(BF16)
        kind = dot(jnp.broadcast_to(late_row(7), (8, 256)).astype(BF16), here, NN)[:1]
        z = last[:LANES]
        for k in range(1, KINDS):
            z = jnp.where(kind == float(k), last[k * LANES : (k + 1) * LANES], z)
        set_basis_out(z)

    def beside_third(i):
        if i < 6:
            set_late_kinds(1 + i)
        if i == 4:
            pick_last_kind()

    for part in range(parts):
        if part > 0:
            wait_all(arrived[part], recv_sem.at[part])
        x = on_halves(
            [None] + list(range(8, 14)),
            part,
            nothing if part else beside_third,
            lambda h: arrived[part][64 * h : 64 * h + 64, :V, :],
        )
        evaluate(part, x.reshape(128 * V, LANES))

    for part in range(parts):
        wait_all(sent[part], send_sem.at[part])


def solution(mesh):
    src_size, tgt_size = mesh.shape["src"], mesh.shape["tgt"]
    devices = src_size * tgt_size
    parts, lag = 2, 3

    def on_device(src_values, src_offset, src_box, tgt_offset, tgt_box, pattern, operators):
        funcs, points = src_values.shape
        V = funcs // parts
        vmem = pl.BlockSpec(memory_space=pltpu.VMEM)
        blocks = [pltpu.VMEM((devices, V + (part == 0), LANES), F32) for part in range(parts)]
        return pl.pallas_call(
            functools.partial(kernel, V, parts, lag, src_size, tgt_size),
            out_shape=jax.ShapeDtypeStruct((funcs, points), F32),
            in_specs=[vmem] * 6 + [pl.BlockSpec(memory_space=pl.ANY)],
            out_specs=vmem,
            scratch_shapes=[
                pltpu.VMEM((15, KINDS * LANES, LANES), F32),
                pltpu.VMEM((15, KINDS * LANES, 3 * LANES), BF16),
                pltpu.VMEM((KINDS * LANES, points), F32),
                pltpu.VMEM((15, 128, LANES), F32),
                pltpu.VMEM((parts, 2, 2, 64, V, LANES), F32),
                pltpu.VMEM((2 * LANES, points), BF16),
                pltpu.VMEM((3 * LANES, points), BF16),
                blocks,
                blocks,
                pltpu.SemaphoreType.DMA((15,)),
                pltpu.SemaphoreType.DMA((parts,)),
                pltpu.SemaphoreType.DMA((parts,)),
            ],
            compiler_params=pltpu.CompilerParams(
                collective_id=0, has_side_effects=True, vmem_limit_bytes=56 * 2**20
            ),
        )(
            src_values,
            src_offset.reshape(1, points),
            src_box.reshape(1, points),
            tgt_offset.reshape(1, points),
            tgt_box.reshape(1, points),
            pattern,
            operators.reshape(15, KINDS * LANES, LANES),
        )

    placed = (
        P(None, ("src", "tgt")),
        P(("src", "tgt")),
        P(("src", "tgt")),
        P(("src", "tgt")),
        P(("src", "tgt")),
        P(None, ("src", "tgt")),
        P(),
    )
    return jax.shard_map(
        on_device, mesh=mesh, in_specs=placed, out_specs=P(None, ("src", "tgt")), check_vma=False
    )
```
